256 devices in a mesh: node: 32 (over y_lo, z, core), local: 8 (over x, y_hi).
Axes of the slice: x: 4, y: 4 (y_hi: 2, y_lo: 2; y = y_hi * 2 + y_lo), z: 8, core: 2. Of those that a mesh axis runs over, the one named last changes fastest.
Arguments:
- acts: bfloat16 [32768, 4096], P(('node', 'local')), may hold values from -6 to 6
- grads_out: bfloat16 [32768, 8192], P(('node', 'local')), may hold values from -6 to 6
- base_output_weight: bfloat16 [4096, 8192], P('local', 'node'), may hold values from -0.09375 to 0.09375
- down_adapter_matrix: bfloat16 [16, 4096], replicated, may hold values from -0.09375 to 0.09375
- b_up: bfloat16 [16, 8192], replicated, may hold values from -0.0625 to 0.0625
Outputs:
- input_activation_gradient: bfloat16 [32768, 4096], P(('node', 'local'))
- grad_down: float32 [16, 4096], replicated
- grad_up: float32 [16, 8192], replicated
The draws below stay inside these ranges and needn't reach their ends.
All inputs are finite; a program needn't handle non-finite values.
Results may differ from the reference program's by a relative error of at most 0.0034.
Values may be sent and summed in bfloat16 or wider, within the bound.
No kernel may reach another device: no remote copies, remote signals or barrier semaphores. Data moves between devices by JAX's collectives and lax.ppermute only.
A program may use at most 128 MiB of HBM per device.

```python
import math
import jax
import jax.numpy as jnp

D = 8192
HD = 4096
R = 16
TOKENS = 32768


def level_of(stream_key, extent, cuts, least, top_value):
    def one(axis_at, blocks):
        draws = jax.random.uniform(jax.random.fold_in(jax.random.fold_in(stream_key, 6), axis_at), (blocks,), jnp.float32, least / len(cuts), top_value / len(cuts))
        return jnp.repeat(jnp.exp(draws), extent[axis_at] // blocks).reshape((-1,) + (1,) * (len(extent) - axis_at - 1))

    factor_of = one(*cuts[0])
    for cut in cuts[1:]:
        factor_of = factor_of * one(*cut)
    return factor_of


def noise(stream_key, shape, scale, limit, split=(), kind=jnp.bfloat16):
    array = scale * jax.random.normal(stream_key, shape, jnp.float32)
    if split:
        array = array * level_of(stream_key, shape, split, -0.22, 0.18)
    return jnp.clip(array, -limit, limit).astype(kind)


def setup_inputs(seed: int = 0) -> dict:
    splits = jax.random.split(jax.random.key(seed), 6)
    acts = noise(splits[0], (TOKENS, HD), 1.0, 6.0, ((0, 256),))
    grads_out = noise(splits[1], (TOKENS, D), 1.0, 6.0, ((0, 256),))
    base_output_weight = noise(splits[2], (HD, D), HD ** -0.5, 0.09375, ((0, 8), (1, 32)))
    down_adapter_matrix = noise(splits[3], (R, HD), HD ** -0.5, 0.09375)
    b_up = noise(splits[4], (R, D), D ** -0.5, 0.0625)
    return dict(acts=acts, grads_out=grads_out, base_output_weight=base_output_weight, down_adapter_matrix=down_adapter_matrix, b_up=b_up)


def reference(acts, grads_out, base_output_weight, down_adapter_matrix, b_up):
    norm_factor = 2.0 / math.sqrt(TOKENS)
    low = jnp.dot(acts, down_adapter_matrix.T, preferred_element_type=jnp.float32).astype(jnp.bfloat16)
    backward_lowrank = jnp.dot(grads_out, b_up.T, preferred_element_type=jnp.float32).astype(jnp.bfloat16)
    grad_down = norm_factor * jnp.dot(backward_lowrank.T, acts, preferred_element_type=jnp.float32)
    grad_up = norm_factor * jnp.dot(low.T, grads_out, preferred_element_type=jnp.float32)
    frozen_contribution = jnp.dot(grads_out, base_output_weight.T, preferred_element_type=jnp.float32)
    lowrank_contribution = 2.0 * jnp.dot(backward_lowrank, down_adapter_matrix, preferred_element_type=jnp.float32)
    input_activation_gradient = (frozen_contribution + lowrank_contribution).astype(jnp.bfloat16)
    return (input_activation_gradient, grad_down, grad_up)
```

```python
import math

import jax
import jax.numpy as jnp
from jax import lax
from jax.sharding import Mesh, PartitionSpec as P

Y = ("yhi", "ylo")
GROUP = ("yhi", "ylo", "core")
REST = ("x", "z")
TOKENS = ("ylo", "z", "core", "x", "yhi")


def gather_by_exchange(value, axes, n):
    return lax.all_to_all(jnp.broadcast_to(value[None], (n, *value.shape)), axes, 0, 0, tiled=True)


def reduce_adapter(part_down, part_up):
    rank = part_down.shape[0]
    both = jnp.concatenate([part_down, part_up], axis=1)
    width = both.shape[1]
    both = both.reshape(rank, 8, width // 8).transpose(1, 0, 2)
    mine = jnp.sum(lax.all_to_all(both, GROUP, 0, 0, tiled=True), axis=0)
    mine = mine.reshape(32, 1, rank * width // 256)
    mine = jnp.sum(lax.all_to_all(mine, REST, 0, 0, tiled=True), axis=0)
    mine = gather_by_exchange(mine, REST, 32).reshape(rank, width // 8)
    both = gather_by_exchange(mine, GROUP, 8)
    both = both.transpose(1, 0, 2).reshape(rank, width)
    return both[:, : part_down.shape[1]], both[:, part_down.shape[1] :]


def local(acts, grads_out, base_output_weight, down_adapter_matrix, b_up):
    rows, hd = acts.shape
    d = grads_out.shape[1]
    norm_factor = 2.0 / math.sqrt(rows * 256)
    w = lax.all_to_all(base_output_weight, "core", split_axis=0, concat_axis=1, tiled=True)
    w = lax.all_gather(w, REST, axis=0, tiled=False)
    w = w.reshape(4, 8, *w.shape[1:])
    halves = grads_out.reshape(rows, 2, d // 2).transpose(1, 0, 2)
    halves = jnp.broadcast_to(halves[None], (2, 2, rows, d // 2)).reshape(4, rows, d // 2)
    g = lax.all_to_all(halves, Y, 0, 0, tiled=True)

    low = jnp.einsum("tk,rk->tr", acts, down_adapter_matrix, preferred_element_type=jnp.float32).astype(jnp.bfloat16)
    back_low = jnp.einsum("td,rd->tr", grads_out, b_up, preferred_element_type=jnp.float32).astype(jnp.bfloat16)
    part_down = norm_factor * jnp.einsum("tr,tk->rk", back_low, acts, preferred_element_type=jnp.float32)
    part_up = norm_factor * jnp.einsum("tr,td->rd", low, grads_out, preferred_element_type=jnp.float32)
    grad_down, grad_up = reduce_adapter(part_down, part_up)
    lowrank = 2.0 * jnp.dot(back_low, down_adapter_matrix, preferred_element_type=jnp.float32)

    g = lax.all_gather(g, "core", axis=1, tiled=False)
    g = g.reshape(8 * rows, 8, d // 16)
    part = jnp.einsum("tzd,xzkd->txk", g, w, preferred_element_type=jnp.float32)
    part = part.astype(jnp.bfloat16).reshape(8, rows, hd // 4)
    part = lax.all_to_all(part, GROUP, 0, 0, tiled=True)
    part = part.reshape(2, 2, 2, rows, 4, hd // 16).astype(jnp.float32)
    frozen = (part[:, 0] + part[:, 1]).transpose(2, 3, 0, 1, 4).reshape(rows, hd)
    return (frozen + lowrank).astype(jnp.bfloat16), grad_down, grad_up


def solution(mesh):
    fine = Mesh(mesh.devices.reshape(2, 8, 2, 4, 2), ("ylo", "z", "core", "x", "yhi"))
    in_specs = (
        P(TOKENS, None),
        P(TOKENS, None),
        P(("x", "yhi"), ("ylo", "z", "core")),
        P(),
        P(),
    )
    out_specs = (P(TOKENS, None), P(), P())
    return jax.shard_map(local, mesh=fine, in_specs=in_specs, out_specs=out_specs, check_vma=False)
```

```python
import functools
import math

import jax
import jax.numpy as jnp
from jax import lax
from jax.experimental import pallas as pl
from jax.experimental.pallas import tpu as pltpu
from jax.sharding import Mesh, PartitionSpec as P

GROUP = ("yhi", "ylo", "core")
REST = ("x", "z")
TOKENS = ("ylo", "z", "core", "x", "yhi")
HOPS = {4: (0, 1, 3, 2)}
F32 = jnp.float32


def place_of(y):
    return 2 * (y % 2) + y // 2


def gather_by_exchange(value, axes, n):
    return lax.all_to_all(jnp.broadcast_to(value[None], (n, *value.shape)), axes, 0, 0, tiled=True)


def swap_cores(value):
    return lax.ppermute(value, "core", [(0, 1), (1, 0)])


def scatter_adapter(part_down, part_up):
    rank = part_down.shape[0]
    both = jnp.concatenate([part_down, part_up], axis=1)
    width = both.shape[1]
    both = both.reshape(rank, 8, width // 8).transpose(1, 0, 2)
    mine = jnp.sum(lax.all_to_all(both, GROUP, 0, 0, tiled=True), axis=0)
    return lax.all_to_all(mine.reshape(32, 1, rank * width // 256), REST, 0, 0, tiled=True)


def gather_adapter(terms, rank, split):
    width = terms.size * 8 // rank
    mine = gather_by_exchange(jnp.sum(terms, axis=0), REST, 32).reshape(rank, width // 8)
    both = gather_by_exchange(mine, GROUP, 8)
    both = both.transpose(1, 0, 2).reshape(rank, width)
    return both[:, :split], both[:, split:]


def product_kernel(place, *refs):
    blocks, (w, out, a_all, w_all, a_sem, w_sem) = refs[:8], refs[8:]
    rows = blocks[0].shape[0]
    kc, depth = w.shape[-2:]

    def w_copies(x):
        return [
            pltpu.make_async_copy(w.at[x, z], w_all.at[pl.ds(x * kc, kc), pl.ds(z * depth, depth)], w_sem.at[8 * x + z])
            for z in range(8)
        ]

    def a_copies(i):
        for j, half in ((i, place[4]), (4 + i, place[5])):
            at = pl.multiple_of((2 * i + half) * rows, rows)
            yield pltpu.make_async_copy(blocks[j], a_all.at[pl.ds(at, rows)], a_sem.at[j])

    for copies in (w_copies(0), w_copies(1), a_copies(0), a_copies(1), a_copies(2), a_copies(3), w_copies(2), w_copies(3)):
        for copy in copies:
            copy.start()
    for side in range(2):
        for copy in w_copies(2 * side) + w_copies(2 * side + 1):
            copy.wait()
        columns = slice(2 * side * kc, 2 * side * kc + 2 * kc)

        @pl.loop(0, 2)
        def _(m):
            if side == 0:

                @pl.loop(0, 2)
                def _(i):
                    for j in (2 * m + i, 4 + 2 * m + i):
                        pltpu.make_async_copy(blocks[0], a_all.at[pl.ds(0, rows)], a_sem.at[j]).wait()

            a = a_all[pl.ds(pl.multiple_of(m * 4 * rows, 4 * rows), 4 * rows)]
            part = lax.dot_general(a, w_all[columns], (((1,), (1,)), ((), ())), preferred_element_type=F32)
            part = part.astype(jnp.bfloat16)
            for i in range(2):
                owner = place[2 * m + i]
                out[2 * owner, :, columns] = part[2 * i * rows : (2 * i + 1) * rows]
                out[2 * owner + 1, :, columns] = part[(2 * i + 1) * rows : (2 * i + 2) * rows]


def product(place, blocks, w):
    rows, k = blocks[0].shape
    kc = w.shape[-2]
    return pl.pallas_call(
        product_kernel,
        out_shape=jax.ShapeDtypeStruct((8, rows, 4 * kc), jnp.bfloat16),
        in_specs=[pl.BlockSpec(memory_space=pltpu.SMEM)] + [pl.BlockSpec(memory_space=pl.ANY)] * 9,
        out_specs=pl.BlockSpec(memory_space=pltpu.VMEM),
        scratch_shapes=[
            pltpu.VMEM((8 * rows, k), jnp.bfloat16),
            pltpu.VMEM((4 * kc, k), jnp.bfloat16),
            pltpu.SemaphoreType.DMA((8,)),
            pltpu.SemaphoreType.DMA((32,)),
        ],
        compiler_params=pltpu.CompilerParams(vmem_limit_bytes=48 * 2**20),
        cost_estimate=pl.CostEstimate(
            flops=64 * rows * kc * k, bytes_accessed=2 * (8 * rows * k + 4 * kc * k + 32 * rows * kc), transcendentals=0
        ),
    )(place, *blocks, w)


def finish_kernel(*refs):
    parts, back_low, down, out = refs[:-3], *refs[-3:]
    back = back_low[...]
    for yhi in range(2):
        for core in range(2):
            one, two = 4 * yhi + core, 4 * yhi + 2 + core
            sums = [p[one].astype(F32) + p[two].astype(F32) for p in parts]
            for x in range(4):
                cols = pl.ds(x * 1024 + yhi * 512 + core * 256, 256)
                frozen = [s[:, x * (s.shape[1] // 4) : (x + 1) * (s.shape[1] // 4)] for s in sums]
                frozen = jnp.concatenate(frozen, axis=1) if len(frozen) > 1 else frozen[0]
                lowrank = 2.0 * jnp.dot(back, down[:, cols], preferred_element_type=F32)
                out[:, cols] = (frozen + lowrank).astype(out.dtype)


def finish(parts, back_low, down):
    rows, rank = back_low.shape
    hd = down.shape[1]
    step = rows // 4
    return pl.pallas_call(
        finish_kernel,
        grid=(4,),
        out_shape=jax.ShapeDtypeStruct((rows, hd), jnp.bfloat16),
        in_specs=[pl.BlockSpec((8, step, p.shape[2]), lambda i: (0, i, 0)) for p in parts]
        + [pl.BlockSpec((step, rank), lambda i: (i, 0)), pl.BlockSpec((rank, hd), lambda i: (0, 0))],
        out_specs=pl.BlockSpec((step, hd), lambda i: (i, 0)),
        compiler_params=pltpu.CompilerParams(vmem_limit_bytes=32 * 2**20),
        cost_estimate=pl.CostEstimate(flops=2 * rows * rank * hd, bytes_accessed=6 * rows * hd, transcendentals=0),
    )(*parts, back_low, down)


def local(acts, grads_out, base_output_weight, down_adapter_matrix, b_up):
    rows, hd = acts.shape
    d = grads_out.shape[1]
    norm_factor = 2.0 / math.sqrt(rows * 256)
    ylo, core = lax.axis_index("ylo"), lax.axis_index("core")
    y = 2 * lax.axis_index("yhi") + ylo
    half = base_output_weight.shape[0] // 2
    mine = lax.dynamic_slice_in_dim(base_output_weight, core * half, half, 0)
    other = swap_cores(lax.dynamic_slice_in_dim(base_output_weight, (1 - core) * half, half, 0))
    w = jnp.where(core == 0, jnp.concatenate([mine, other], axis=1), jnp.concatenate([other, mine], axis=1))
    w = lax.all_gather(w, REST, axis=0, tiled=False).reshape(4, 8, *w.shape)
    keep = lax.dynamic_slice_in_dim(grads_out, ylo * (d // 2), d // 2, 1)
    give = lax.dynamic_slice_in_dim(grads_out, (1 - ylo) * (d // 2), d // 2, 1)
    blocks = [keep]
    for hop, value in zip(HOPS[4][1:], (give, give, keep)):
        blocks.append(lax.ppermute(value, ("ylo", "yhi"), [(place_of(i), place_of((i + hop) % 4)) for i in range(4)]))
    blocks += [swap_cores(b) for b in blocks]
    from_y = (y - jnp.array(HOPS[4])) % 4
    place = jnp.concatenate([from_y, jnp.stack([core, 1 - core])]).astype(jnp.int32)

    low = jnp.einsum("tk,rk->tr", acts, down_adapter_matrix, preferred_element_type=F32).astype(jnp.bfloat16)
    back_low = jnp.einsum("td,rd->tr", grads_out, b_up, preferred_element_type=F32).astype(jnp.bfloat16)
    part_down = norm_factor * jnp.einsum("tr,tk->rk", back_low, acts, preferred_element_type=F32)
    part_up = norm_factor * jnp.einsum("tr,td->rd", low, grads_out, preferred_element_type=F32)
    terms = scatter_adapter(part_down, part_up)

    parts = [product(place, blocks, w)]
    parts = [lax.all_to_all(p, GROUP, 0, 0, tiled=True) for p in parts]
    grad_down, grad_up = gather_adapter(terms, low.shape[1], hd)
    return finish(parts, back_low, down_adapter_matrix), grad_down, grad_up


def solution(mesh):
    fine = Mesh(mesh.devices.reshape(2, 8, 2, 4, 2), ("ylo", "z", "core", "x", "yhi"))
    in_specs = (
        P(TOKENS, None),
        P(TOKENS, None),
        P(("x", "yhi"), ("ylo", "z", "core")),
        P(),
        P(),
    )
    out_specs = (P(TOKENS, None), P(), P())
    return jax.shard_map(local, mesh=fine, in_specs=in_specs, out_specs=out_specs, check_vma=False)
```

```python
import functools
import math

import jax
import jax.numpy as jnp
from jax import lax
from jax.experimental import pallas as pl
from jax.experimental.pallas import tpu as pltpu
from jax.sharding import Mesh, PartitionSpec as P

Y = ("yhi", "ylo")
GROUP = ("yhi", "ylo", "core")
REST = ("x", "z")
TOKENS = ("ylo", "z", "core", "x", "yhi")
HOPS = (0, 1, 3, 2)
F32 = jnp.float32


def place_of(y):
    return 2 * (y % 2) + y // 2


def gather_by_exchange(value, axes, n):
    return lax.all_to_all(jnp.broadcast_to(value[None], (n, *value.shape)), axes, 0, 0, tiled=True)


def along_y(value, hop):
    return lax.ppermute(value, ("ylo", "yhi"), [(place_of(i), place_of((i + hop) % 4)) for i in range(4)])


def scatter_group(part_down, part_up):
    rank = part_down.shape[0]
    both = jnp.concatenate([part_down, part_up], axis=1)
    width = both.shape[1]
    both = both.reshape(rank, 8, width // 8).transpose(1, 0, 2)
    return jnp.sum(lax.all_to_all(both, GROUP, 0, 0, tiled=True), axis=0)


def scatter_rest(mine):
    return lax.all_to_all(mine.reshape(32, 1, mine.size // 32), REST, 0, 0, tiled=True)


def gather_adapter(terms, rank, split):
    width = terms.size * 8 // rank
    mine = gather_by_exchange(jnp.sum(terms, axis=0), REST, 32).reshape(rank, width // 8)
    both = gather_by_exchange(mine, GROUP, 8)
    both = both.transpose(1, 0, 2).reshape(rank, width)
    return both[:, :split], both[:, split:]


def product_kernel(owner, *refs):
    blocks, (w, out, a_all, w_all, total, a_sem, w_sem) = refs[:4], refs[4:]
    rows, k = blocks[0].shape
    parts, _, kc, depth = w.shape
    wide = depth // 2

    def copies(i):
        yield pltpu.make_async_copy(w.at[i], w_all.at[i], w_sem.at[i])
        for j, block in enumerate(blocks):
            for ylo in range(2):
                source = block.at[:, pl.ds(pl.multiple_of(ylo * (k // 2) + i * wide, wide), wide)]
                target = a_all.at[i, pl.ds(j * rows, rows), pl.ds(ylo * wide, wide)]
                yield pltpu.make_async_copy(source, target, a_sem.at[i, 2 * j + ylo])

    @pl.loop(0, parts)
    def _(i):
        for copy in copies(i):
            copy.start()

    def terms(step):
        for q in range(2):
            for copy in copies(2 * step + q):
                copy.wait()
        return sum(
            lax.dot_general(
                a_all[2 * step + q],
                w_all[2 * step + q].reshape(4 * kc, depth),
                (((1,), (1,)), ((), ())),
                preferred_element_type=F32,
            )
            for q in range(2)
        )

    total[...] = terms(0)

    @pl.loop(1, parts // 2)
    def _(step):
        total[...] += terms(step)

    for j in range(4):
        out[owner[j]] = total[j * rows : (j + 1) * rows].astype(out.dtype)


def product(owner, blocks, w):
    rows, k = blocks[0].shape
    parts, _, kc, depth = w.shape
    return pl.pallas_call(
        product_kernel,
        out_shape=jax.ShapeDtypeStruct((4, rows, 4 * kc), jnp.bfloat16),
        in_specs=[pl.BlockSpec(memory_space=pltpu.SMEM)] + [pl.BlockSpec(memory_space=pl.ANY)] * 5,
        out_specs=pl.BlockSpec(memory_space=pltpu.VMEM),
        scratch_shapes=[
            pltpu.VMEM((parts, 4 * rows, depth), jnp.bfloat16),
            pltpu.VMEM((parts, 4, kc, depth), jnp.bfloat16),
            pltpu.VMEM((4 * rows, 4 * kc), F32),
            pltpu.SemaphoreType.DMA((parts, 8)),
            pltpu.SemaphoreType.DMA((parts,)),
        ],
        compiler_params=pltpu.CompilerParams(vmem_limit_bytes=48 * 2**20),
        cost_estimate=pl.CostEstimate(
            flops=32 * rows * kc * k, bytes_accessed=2 * (4 * rows * k + 4 * kc * k + 16 * rows * kc), transcendentals=0
        ),
    )(owner, *blocks, w)


def finish_kernel(parts, back_low, down, out):
    kc = parts.shape[2] // 4
    lowrank = 2.0 * jnp.dot(back_low[...], down[...], preferred_element_type=F32)
    for x in range(4):
        for y in range(4):
            columns = slice((4 * x + y) * kc, (4 * x + y + 1) * kc)
            frozen = parts[y, :, x * kc : (x + 1) * kc].astype(F32)
            out[:, columns] = (frozen + lowrank[:, columns]).astype(out.dtype)


def finish(parts, back_low, down):
    rows, rank = back_low.shape
    hd = down.shape[1]
    step = rows // 4
    return pl.pallas_call(
        finish_kernel,
        grid=(4,),
        out_shape=jax.ShapeDtypeStruct((rows, hd), jnp.bfloat16),
        in_specs=[
            pl.BlockSpec((4, step, hd // 4), lambda i: (0, i, 0)),
            pl.BlockSpec((step, rank), lambda i: (i, 0)),
            pl.BlockSpec((rank, hd), lambda i: (0, 0)),
        ],
        out_specs=pl.BlockSpec((step, hd), lambda i: (i, 0)),
        compiler_params=pltpu.CompilerParams(vmem_limit_bytes=32 * 2**20),
        cost_estimate=pl.CostEstimate(flops=2 * rows * rank * hd, bytes_accessed=4 * rows * hd, transcendentals=0),
    )(parts, back_low, down)


def local(acts, grads_out, base_output_weight, down_adapter_matrix, b_up):
    rows, hd = acts.shape
    d = grads_out.shape[1]
    norm_factor = 2.0 / math.sqrt(rows * 256)
    ylo = lax.axis_index("ylo")
    y = 2 * lax.axis_index("yhi") + ylo
    half = base_output_weight.shape[0] // 2
    mine = lax.dynamic_slice_in_dim(base_output_weight, ylo * half, half, 0)
    other = lax.dynamic_slice_in_dim(base_output_weight, (1 - ylo) * half, half, 0)
    other = lax.ppermute(other, "ylo", [(0, 1), (1, 0)])
    w = jnp.where(ylo == 0, jnp.concatenate([mine, other], axis=1), jnp.concatenate([other, mine], axis=1))
    w = lax.all_gather(w, ("z", "core", "x"), axis=0, tiled=False).reshape(16, 4, *w.shape)
    near = [along_y(grads_out, hop) for hop in HOPS[1:3]]

    low = jnp.einsum("tk,rk->tr", acts, down_adapter_matrix, preferred_element_type=F32).astype(jnp.bfloat16)
    back_low = jnp.einsum("td,rd->tr", grads_out, b_up, preferred_element_type=F32).astype(jnp.bfloat16)
    part_down = norm_factor * jnp.einsum("tr,tk->rk", back_low, acts, preferred_element_type=F32)
    part_up = norm_factor * jnp.einsum("tr,td->rd", low, grads_out, preferred_element_type=F32)
    total = scatter_group(part_down, part_up)
    total, far, *near = lax.optimization_barrier((total, grads_out, *near))
    blocks = [grads_out, *near, along_y(far, HOPS[3])]
    terms = scatter_rest(total)

    parts = product(((y - jnp.array(HOPS)) % 4).astype(jnp.int32), blocks, w)
    parts = lax.all_to_all(parts, Y, 0, 0, tiled=True)
    grad_down, grad_up = gather_adapter(terms, low.shape[1], hd)
    return finish(parts, back_low, down_adapter_matrix), grad_down, grad_up


def solution(mesh):
    fine = Mesh(mesh.devices.reshape(2, 8, 2, 4, 2), ("ylo", "z", "core", "x", "yhi"))
    in_specs = (
        P(TOKENS, None),
        P(TOKENS, None),
        P(("x", "yhi"), ("ylo", "z", "core")),
        P(),
        P(),
    )
    out_specs = (P(TOKENS, None), P(), P())
    return jax.shard_map(local, mesh=fine, in_specs=in_specs, out_specs=out_specs, check_vma=False)
```

```python
import functools
import math

import jax
import jax.numpy as jnp
from jax import lax
from jax.experimental import pallas as pl
from jax.experimental.pallas import tpu as pltpu
from jax.sharding import Mesh, PartitionSpec as P

GROUP = ("yhi", "ylo", "core")
REST = ("x", "z")
TOKENS = ("ylo", "z", "core", "x", "yhi")
HOPS = (0, 1, 3, 2)
F32 = jnp.float32


def place_of(y):
    return 2 * (y % 2) + y // 2


def gather_by_exchange(value, axes, n):
    return lax.all_to_all(jnp.broadcast_to(value[None], (n, *value.shape)), axes, 0, 0, tiled=True)


def along_y(value, hop):
    return lax.ppermute(value, ("ylo", "yhi"), [(place_of(i), place_of((i + hop) % 4)) for i in range(4)])


def scatter_group(part_down, part_up):
    rank = part_down.shape[0]
    both = jnp.concatenate([part_down, part_up], axis=1)
    width = both.shape[1]
    both = both.reshape(rank, 8, width // 8).transpose(1, 0, 2)
    return jnp.sum(lax.all_to_all(both, GROUP, 0, 0, tiled=True), axis=0)


def scatter_rest(mine):
    return lax.all_to_all(mine.reshape(32, 1, mine.size // 32), REST, 0, 0, tiled=True)


def gather_adapter(terms, rank, split):
    width = terms.size * 8 // rank
    mine = gather_by_exchange(jnp.sum(terms, axis=0), REST, 32).reshape(rank, width // 8)
    both = gather_by_exchange(mine, GROUP, 8)
    both = both.transpose(1, 0, 2).reshape(rank, width)
    return both[:, :split], both[:, split:]


def product_kernel(count, *refs):
    blocks, w, outs, (a_all, w_all, total, a_sem, w_sem) = refs[:count], refs[count], refs[count + 1 : 2 * count + 1], refs[2 * count + 1 :]
    rows, k = blocks[0].shape
    parts, _, kc, depth = w.shape
    wide = depth // 2

    def w_copy(i):
        return pltpu.make_async_copy(w.at[i], w_all.at[i], w_sem.at[i])

    def a_copies(part):
        for j, block in enumerate(blocks):
            for ylo in range(2):
                columns = pl.ds(ylo * (k // 2) + part * 4 * wide, 4 * wide)
                target = a_all.at[pl.ds(j * rows, rows), columns]
                yield pltpu.make_async_copy(block.at[:, columns], target, a_sem.at[part, 2 * j + ylo])

    for part in range(parts // 4):
        for copy in a_copies(part):
            copy.start()
        for i in range(4):
            w_copy(4 * part + i).start()

    def term(i, ylo):
        a = a_all[:, pl.ds(pl.multiple_of(ylo * (k // 2) + i * wide, wide), wide)]
        b = w_all[i, :, :, ylo * wide : (ylo + 1) * wide].reshape(4 * kc, wide)
        return lax.dot_general(a, b, (((1,), (1,)), ((), ())), preferred_element_type=F32)

    for part in range(parts // 4):
        for copy in a_copies(part):
            copy.wait()

        @pl.loop(0, 2)
        def _(half):
            first = 4 * part + 2 * half
            for i in range(2):
                w_copy(first + i).wait()
            here = sum(term(first + i, ylo) for i in range(2) for ylo in range(2))
            if part == 0:

                @pl.when(half == 0)
                def _():
                    total[...] = here

                @pl.when(half == 1)
                def _():
                    total[...] += here

            else:
                total[...] += here

    for j, out in enumerate(outs):
        out[...] = total[j * rows : (j + 1) * rows].astype(out.dtype)


def product(blocks, w):
    rows, k = blocks[0].shape
    parts, _, kc, depth = w.shape
    n = len(blocks)
    return pl.pallas_call(
        functools.partial(product_kernel, n),
        out_shape=[jax.ShapeDtypeStruct((rows, 4 * kc), jnp.bfloat16)] * n,
        in_specs=[pl.BlockSpec(memory_space=pl.ANY)] * (n + 1),
        out_specs=[pl.BlockSpec(memory_space=pltpu.VMEM)] * n,
        scratch_shapes=[
            pltpu.VMEM((n * rows, k), jnp.bfloat16),
            pltpu.VMEM((parts, 4, kc, depth), jnp.bfloat16),
            pltpu.VMEM((n * rows, 4 * kc), F32),
            pltpu.SemaphoreType.DMA((parts // 4, 2 * n)),
            pltpu.SemaphoreType.DMA((parts,)),
        ],
        compiler_params=pltpu.CompilerParams(vmem_limit_bytes=48 * 2**20),
        cost_estimate=pl.CostEstimate(
            flops=8 * n * rows * kc * k,
            bytes_accessed=2 * (n * rows * k + 4 * kc * k + 4 * n * rows * kc),
            transcendentals=0,
        ),
    )(*blocks, w)


def finish_kernel(place, *refs):
    parts, (back_low, down, out) = refs[:4], refs[4:]
    kc = parts[0].shape[1] // 4
    lowrank = 2.0 * jnp.dot(back_low[...], down[...], preferred_element_type=F32)
    for y in range(4):

        @pl.when(place[0] == y)
        def _():
            for hop, part in zip(HOPS, parts):
                for x in range(4):
                    at = (4 * x + (y + hop) % 4) * kc
                    columns = slice(at, at + kc)
                    frozen = part[:, x * kc : (x + 1) * kc].astype(F32)
                    out[:, columns] = (frozen + lowrank[:, columns]).astype(out.dtype)


def finish(place, parts, back_low, down):
    rows, rank = back_low.shape
    hd = down.shape[1]
    step = rows // 4
    return pl.pallas_call(
        finish_kernel,
        grid=(4,),
        out_shape=jax.ShapeDtypeStruct((rows, hd), jnp.bfloat16),
        in_specs=[pl.BlockSpec(memory_space=pltpu.SMEM)]
        + [pl.BlockSpec((step, hd // 4), lambda i: (i, 0))] * 4
        + [pl.BlockSpec((step, rank), lambda i: (i, 0)), pl.BlockSpec((rank, hd), lambda i: (0, 0))],
        out_specs=pl.BlockSpec((step, hd), lambda i: (i, 0)),
        compiler_params=pltpu.CompilerParams(vmem_limit_bytes=32 * 2**20),
        cost_estimate=pl.CostEstimate(flops=2 * rows * rank * hd, bytes_accessed=4 * rows * hd, transcendentals=0),
    )(place, *parts, back_low, down)


def local(acts, grads_out, base_output_weight, down_adapter_matrix, b_up):
    rows, hd = acts.shape
    d = grads_out.shape[1]
    norm_factor = 2.0 / math.sqrt(rows * 256)
    ylo = lax.axis_index("ylo")
    y = 2 * lax.axis_index("yhi") + ylo
    half = base_output_weight.shape[0] // 2
    mine = lax.dynamic_slice_in_dim(base_output_weight, ylo * half, half, 0)
    other = lax.dynamic_slice_in_dim(base_output_weight, (1 - ylo) * half, half, 0)
    other = lax.ppermute(other, "ylo", [(0, 1), (1, 0)])
    w = jnp.where(ylo == 0, jnp.concatenate([mine, other], axis=1), jnp.concatenate([other, mine], axis=1))
    w = lax.all_gather(w, ("z", "core", "x"), axis=0, tiled=False).reshape(16, 4, *w.shape)
    near = [along_y(grads_out, hop) for hop in HOPS[1:3]]

    low = jnp.einsum("tk,rk->tr", acts, down_adapter_matrix, preferred_element_type=F32).astype(jnp.bfloat16)
    back_low = jnp.einsum("td,rd->tr", grads_out, b_up, preferred_element_type=F32).astype(jnp.bfloat16)
    part_down = norm_factor * jnp.einsum("tr,tk->rk", back_low, acts, preferred_element_type=F32)
    part_up = norm_factor * jnp.einsum("tr,td->rd", low, grads_out, preferred_element_type=F32)
    total = scatter_group(part_down, part_up)
    total, far, *near = lax.optimization_barrier((total, grads_out, *near))
    blocks = [grads_out, *near, along_y(far, HOPS[3])]
    terms = scatter_rest(total)

    own, near_up, near_down, far = blocks
    from_far, from_up, from_down = product([far, near_up, near_down], w)
    (from_own,) = product([own], w)
    parts = [from_own, along_y(from_up, HOPS[2]), along_y(from_down, HOPS[1]), along_y(from_far, HOPS[3])]
    place = y.astype(jnp.int32)[None]
    grad_down, grad_up = gather_adapter(terms, low.shape[1], hd)
    return finish(place, parts, back_low, down_adapter_matrix), grad_down, grad_up


def solution(mesh):
    fine = Mesh(mesh.devices.reshape(2, 8, 2, 4, 2), ("ylo", "z", "core", "x", "yhi"))
    in_specs = (
        P(TOKENS, None),
        P(TOKENS, None),
        P(("x", "yhi"), ("ylo", "z", "core")),
        P(),
        P(),
    )
    out_specs = (P(TOKENS, None), P(), P())
    return jax.shard_map(local, mesh=fine, in_specs=in_specs, out_specs=out_specs, check_vma=False)
```

```python
import functools
import math

import jax
import jax.numpy as jnp
from jax import lax
from jax.experimental import pallas as pl
from jax.experimental.pallas import tpu as pltpu
from jax.sharding import Mesh, PartitionSpec as P

GROUP = ("yhi", "ylo", "core")
REST = ("x", "z")
TOKENS = ("ylo", "z", "core", "x", "yhi")
HOPS = (0, 1, 3, 2)
F32 = jnp.float32


def place_of(y):
    return 2 * (y % 2) + y // 2


def gather_by_exchange(value, axes, n):
    return lax.all_to_all(jnp.broadcast_to(value[None], (n, *value.shape)), axes, 0, 0, tiled=True)


def along_y(value, hop):
    return lax.ppermute(value, ("ylo", "yhi"), [(place_of(i), place_of((i + hop) % 4)) for i in range(4)])


def scatter_group(part_down, part_up):
    rank = part_down.shape[0]
    both = jnp.concatenate([part_down, part_up], axis=1)
    width = both.shape[1]
    both = both.reshape(rank, 8, width // 8).transpose(1, 0, 2)
    return jnp.sum(lax.all_to_all(both, GROUP, 0, 0, tiled=True), axis=0)


def scatter_rest(mine):
    return lax.all_to_all(mine.reshape(32, 1, mine.size // 32), REST, 0, 0, tiled=True)


def gather_adapter(terms, rank, split):
    width = terms.size * 8 // rank
    mine = gather_by_exchange(jnp.sum(terms, axis=0), REST, 32).reshape(rank, width // 8)
    both = gather_by_exchange(mine, GROUP, 8)
    both = both.transpose(1, 0, 2).reshape(rank, width)
    return both[:, :split], both[:, split:]


def product_kernel(count, *refs):
    blocks, w, outs, (a_all, w_all, total, a_sem, w_sem) = refs[:count], refs[count], refs[count + 1 : 2 * count + 1], refs[2 * count + 1 :]
    rows, k = blocks[0].shape
    _, parts, kc, depth = w.shape
    wide = depth // 2

    def w_copy(i):
        return pltpu.make_async_copy(w.at[:, i], w_all.at[i], w_sem.at[i])

    def a_copies(part):
        for j, block in enumerate(blocks):
            for ylo in range(2):
                columns = pl.ds(ylo * (k // 2) + part * 4 * wide, 4 * wide)
                target = a_all.at[pl.ds(j * rows, rows), columns]
                yield pltpu.make_async_copy(block.at[:, columns], target, a_sem.at[part, 2 * j + ylo])

    for part in range(parts // 4):
        for copy in a_copies(part):
            copy.start()
        for i in range(4):
            w_copy(4 * part + i).start()

    def term(i, ylo):
        a = a_all[:, pl.ds(pl.multiple_of(ylo * (k // 2) + i * wide, wide), wide)]
        b = w_all[i, :, :, ylo * wide : (ylo + 1) * wide].reshape(4 * kc, wide)
        return lax.dot_general(a, b, (((1,), (1,)), ((), ())), preferred_element_type=F32)

    for part in range(parts // 4):
        for copy in a_copies(part):
            copy.wait()

        @pl.loop(0, 2)
        def _(half):
            first = 4 * part + 2 * half
            for i in range(2):
                w_copy(first + i).wait()
            here = sum(term(first + i, ylo) for i in range(2) for ylo in range(2))
            if part == 0:

                @pl.when(half == 0)
                def _():
                    total[...] = here

                @pl.when(half == 1)
                def _():
                    total[...] += here

            else:
                total[...] += here

    for j, out in enumerate(outs):
        out[...] = total[j * rows : (j + 1) * rows].astype(out.dtype)


def product(blocks, w):
    rows, k = blocks[0].shape
    _, parts, kc, depth = w.shape
    n = len(blocks)
    return pl.pallas_call(
        functools.partial(product_kernel, n),
        out_shape=[jax.ShapeDtypeStruct((rows, 4 * kc), jnp.bfloat16)] * n,
        in_specs=[pl.BlockSpec(memory_space=pl.ANY)] * (n + 1),
        out_specs=[pl.BlockSpec(memory_space=pltpu.VMEM)] * n,
        scratch_shapes=[
            pltpu.VMEM((n * rows, k), jnp.bfloat16),
            pltpu.VMEM((parts, 4, kc, depth), jnp.bfloat16),
            pltpu.VMEM((n * rows, 4 * kc), F32),
            pltpu.SemaphoreType.DMA((parts // 4, 2 * n)),
            pltpu.SemaphoreType.DMA((parts,)),
        ],
        compiler_params=pltpu.CompilerParams(vmem_limit_bytes=48 * 2**20),
        cost_estimate=pl.CostEstimate(
            flops=8 * n * rows * kc * k,
            bytes_accessed=2 * (n * rows * k + 4 * kc * k + 4 * n * rows * kc),
            transcendentals=0,
        ),
    )(*blocks, w)


def finish_kernel(place, *refs):
    parts, (back_low, down, out) = refs[:4], refs[4:]
    kc = parts[0].shape[1] // 4
    lowrank = 2.0 * jnp.dot(back_low[...], down[...], preferred_element_type=F32)
    for y in range(4):

        @pl.when(place[0] == y)
        def _():
            for hop, part in zip(HOPS, parts):
                for x in range(4):
                    at = (4 * x + (y + hop) % 4) * kc
                    columns = slice(at, at + kc)
                    frozen = part[:, x * kc : (x + 1) * kc].astype(F32)
                    out[:, columns] = (frozen + lowrank[:, columns]).astype(out.dtype)


def finish(place, parts, back_low, down):
    rows, rank = back_low.shape
    hd = down.shape[1]
    step = rows // 2
    return pl.pallas_call(
        finish_kernel,
        grid=(2,),
        out_shape=jax.ShapeDtypeStruct((rows, hd), jnp.bfloat16),
        in_specs=[pl.BlockSpec(memory_space=pltpu.SMEM)]
        + [pl.BlockSpec((step, hd // 4), lambda i: (i, 0))] * 4
        + [pl.BlockSpec((step, rank), lambda i: (i, 0)), pl.BlockSpec((rank, hd), lambda i: (0, 0))],
        out_specs=pl.BlockSpec((step, hd), lambda i: (i, 0)),
        compiler_params=pltpu.CompilerParams(vmem_limit_bytes=32 * 2**20),
        cost_estimate=pl.CostEstimate(flops=2 * rows * rank * hd, bytes_accessed=4 * rows * hd, transcendentals=0),
    )(place, *parts, back_low, down)


def local(acts, grads_out, base_output_weight, down_adapter_matrix, b_up):
    rows, hd = acts.shape
    d = grads_out.shape[1]
    norm_factor = 2.0 / math.sqrt(rows * 256)
    ylo = lax.axis_index("ylo")
    y = 2 * lax.axis_index("yhi") + ylo
    half = base_output_weight.shape[0] // 2
    other = lax.dynamic_slice_in_dim(base_output_weight, (1 - ylo) * half, half, 0)
    other, kept = lax.optimization_barrier((other, base_output_weight))
    mine = lax.dynamic_slice_in_dim(kept, ylo * half, half, 0)
    other = lax.ppermute(other, "ylo", [(0, 1), (1, 0)])
    w = jnp.where(ylo == 0, jnp.concatenate([mine, other], axis=1), jnp.concatenate([other, mine], axis=1))
    w = lax.all_gather(w, ("x", "z", "core"), axis=0, tiled=False).reshape(4, 16, *w.shape)
    near = [along_y(grads_out, hop) for hop in HOPS[1:3]]

    low = jnp.einsum("tk,rk->tr", acts, down_adapter_matrix, preferred_element_type=F32).astype(jnp.bfloat16)
    back_low = jnp.einsum("td,rd->tr", grads_out, b_up, preferred_element_type=F32).astype(jnp.bfloat16)
    part_down = norm_factor * jnp.einsum("tr,tk->rk", back_low, acts, preferred_element_type=F32)
    part_up = norm_factor * jnp.einsum("tr,td->rd", low, grads_out, preferred_element_type=F32)
    total = scatter_group(part_down, part_up)
    total, far, *near = lax.optimization_barrier((total, grads_out, *near))
    blocks = [grads_out, *near, along_y(far, HOPS[3])]
    terms = scatter_rest(total)

    own, near_up, near_down, far = blocks
    from_far, from_up, from_down = product([far, near_up, near_down], w)
    (from_own,) = product([own], w)
    parts = [from_own, along_y(from_up, HOPS[2]), along_y(from_down, HOPS[1]), along_y(from_far, HOPS[3])]
    place = y.astype(jnp.int32)[None]
    grad_down, grad_up = gather_adapter(terms, low.shape[1], hd)
    return finish(place, parts, back_low, down_adapter_matrix), grad_down, grad_up


def solution(mesh):
    fine = Mesh(mesh.devices.reshape(2, 8, 2, 4, 2), ("ylo", "z", "core", "x", "yhi"))
    in_specs = (
        P(TOKENS, None),
        P(TOKENS, None),
        P(("x", "yhi"), ("ylo", "z", "core")),
        P(),
        P(),
    )
    out_specs = (P(TOKENS, None), P(), P())
    return jax.shard_map(local, mesh=fine, in_specs=in_specs, out_specs=out_specs, check_vma=False)
```

```python
import functools
import math

import jax
import jax.numpy as jnp
from jax import lax
from jax.experimental import pallas as pl
from jax.experimental.pallas import tpu as pltpu
from jax.sharding import Mesh, PartitionSpec as P

GROUP = ("core", "yhi", "ylo")
REST = ("x", "z")
TOKENS = ("ylo", "z", "core", "x", "yhi")
HOPS = (0, 1, 3, 2)
F32 = jnp.float32


def place_of(y):
    return 2 * (y % 2) + y // 2


def gather_by_exchange(value, axes, n):
    return lax.all_to_all(jnp.broadcast_to(value[None], (n, *value.shape)), axes, 0, 0, tiled=True)


def along_y(value, hop):
    return lax.ppermute(value, ("ylo", "yhi"), [(place_of(i), place_of((i + hop) % 4)) for i in range(4)])


def scatter_group(part_down, part_up, y, core):
    both = jnp.concatenate([part_down, part_up], axis=1)
    width = both.shape[1] // 8
    at = [4 * core * width, 4 * (1 - core) * width]
    mine, other = (lax.dynamic_slice_in_dim(both, i, 4 * width, 1) for i in at)
    mine = mine + lax.ppermute(other, "core", [(0, 1), (1, 0)])
    total = lax.dynamic_slice_in_dim(mine, y * width, width, 1)
    for hop in HOPS[1:]:
        total = total + along_y(lax.dynamic_slice_in_dim(mine, (y + hop) % 4 * width, width, 1), hop)
    return total


def scatter_rest(mine):
    return lax.all_to_all(mine.reshape(32, 1, mine.size // 32), REST, 0, 0, tiled=True)


def gather_adapter(terms, rank, split):
    width = terms.size * 8 // rank
    mine = gather_by_exchange(jnp.sum(terms, axis=0), REST, 32).reshape(rank, width // 8)
    both = gather_by_exchange(mine, GROUP, 8)
    both = both.transpose(1, 0, 2).reshape(rank, width)
    return both[:, :split], both[:, split:]


def product_kernel(count, *refs):
    blocks, w, outs, (a_all, w_all, total, a_sem, w_sem) = refs[:count], refs[count], refs[count + 1 : 2 * count + 1], refs[2 * count + 1 :]
    rows, k = blocks[0].shape
    _, parts, kc, depth = w.shape
    wide = depth // 2

    def w_copy(i):
        return pltpu.make_async_copy(w.at[:, i], w_all.at[i], w_sem.at[i])

    def a_copies(part):
        for j, block in enumerate(blocks):
            for ylo in range(2):
                columns = pl.ds(ylo * (k // 2) + part * 4 * wide, 4 * wide)
                target = a_all.at[pl.ds(j * rows, rows), columns]
                yield pltpu.make_async_copy(block.at[:, columns], target, a_sem.at[part, 2 * j + ylo])

    for part in range(parts // 4):
        for copy in a_copies(part):
            copy.start()
        for i in range(4):
            w_copy(4 * part + i).start()

    def term(i, ylo):
        a = a_all[:, pl.ds(pl.multiple_of(ylo * (k // 2) + i * wide, wide), wide)]
        b = w_all[i, :, :, ylo * wide : (ylo + 1) * wide].reshape(4 * kc, wide)
        return lax.dot_general(a, b, (((1,), (1,)), ((), ())), preferred_element_type=F32)

    for part in range(parts // 4):
        for copy in a_copies(part):
            copy.wait()

        @pl.loop(0, 2)
        def _(half):
            first = 4 * part + 2 * half
            for i in range(2):
                w_copy(first + i).wait()
            here = sum(term(first + i, ylo) for i in range(2) for ylo in range(2))
            if part == 0:

                @pl.when(half == 0)
                def _():
                    total[...] = here

                @pl.when(half == 1)
                def _():
                    total[...] += here

            else:
                total[...] += here

    for j, out in enumerate(outs):
        out[...] = total[j * rows : (j + 1) * rows].astype(out.dtype)


def product(blocks, w):
    rows, k = blocks[0].shape
    _, parts, kc, depth = w.shape
    n = len(blocks)
    return pl.pallas_call(
        functools.partial(product_kernel, n),
        out_shape=[jax.ShapeDtypeStruct((rows, 4 * kc), jnp.bfloat16)] * n,
        in_specs=[pl.BlockSpec(memory_space=pl.ANY)] * (n + 1),
        out_specs=[pl.BlockSpec(memory_space=pltpu.VMEM)] * n,
        scratch_shapes=[
            pltpu.VMEM((n * rows, k), jnp.bfloat16),
            pltpu.VMEM((parts, 4, kc, depth), jnp.bfloat16),
            pltpu.VMEM((n * rows, 4 * kc), F32),
            pltpu.SemaphoreType.DMA((parts // 4, 2 * n)),
            pltpu.SemaphoreType.DMA((parts,)),
        ],
        compiler_params=pltpu.CompilerParams(vmem_limit_bytes=48 * 2**20),
        cost_estimate=pl.CostEstimate(
            flops=8 * n * rows * kc * k,
            bytes_accessed=2 * (n * rows * k + 4 * kc * k + 4 * n * rows * kc),
            transcendentals=0,
        ),
    )(*blocks, w)


def finish_kernel(place, *refs):
    parts, (back_low, down, out) = refs[:4], refs[4:]
    kc = parts[0].shape[1] // 4
    lowrank = 2.0 * jnp.dot(back_low[...], down[...], preferred_element_type=F32)
    for y in range(4):

        @pl.when(place[0] == y)
        def _():
            for hop, part in zip(HOPS, parts):
                for x in range(4):
                    at = (4 * x + (y + hop) % 4) * kc
                    columns = slice(at, at + kc)
                    frozen = part[:, x * kc : (x + 1) * kc].astype(F32)
                    out[:, columns] = (frozen + lowrank[:, columns]).astype(out.dtype)


def finish(place, parts, back_low, down):
    rows, rank = back_low.shape
    hd = down.shape[1]
    step = rows // 2
    return pl.pallas_call(
        finish_kernel,
        grid=(2,),
        out_shape=jax.ShapeDtypeStruct((rows, hd), jnp.bfloat16),
        in_specs=[pl.BlockSpec(memory_space=pltpu.SMEM)]
        + [pl.BlockSpec((step, hd // 4), lambda i: (i, 0))] * 4
        + [pl.BlockSpec((step, rank), lambda i: (i, 0)), pl.BlockSpec((rank, hd), lambda i: (0, 0))],
        out_specs=pl.BlockSpec((step, hd), lambda i: (i, 0)),
        compiler_params=pltpu.CompilerParams(vmem_limit_bytes=32 * 2**20),
        cost_estimate=pl.CostEstimate(flops=2 * rows * rank * hd, bytes_accessed=4 * rows * hd, transcendentals=0),
    )(place, *parts, back_low, down)


def local(acts, grads_out, base_output_weight, down_adapter_matrix, b_up):
    rows, hd = acts.shape
    d = grads_out.shape[1]
    norm_factor = 2.0 / math.sqrt(rows * 256)
    ylo = lax.axis_index("ylo")
    y = 2 * lax.axis_index("yhi") + ylo
    half = base_output_weight.shape[0] // 2
    other = lax.dynamic_slice_in_dim(base_output_weight, (1 - ylo) * half, half, 0)
    other, kept = lax.optimization_barrier((other, base_output_weight))
    mine = lax.dynamic_slice_in_dim(kept, ylo * half, half, 0)
    other = lax.ppermute(other, "ylo", [(0, 1), (1, 0)])
    w = jnp.where(ylo == 0, jnp.concatenate([mine, other], axis=1), jnp.concatenate([other, mine], axis=1))
    w = lax.all_gather(w, ("x", "z", "core"), axis=0, tiled=False).reshape(4, 16, *w.shape)
    near = [along_y(grads_out, hop) for hop in HOPS[1:3]]

    low = jnp.einsum("tk,rk->tr", acts, down_adapter_matrix, preferred_element_type=F32).astype(jnp.bfloat16)
    back_low = jnp.einsum("td,rd->tr", grads_out, b_up, preferred_element_type=F32).astype(jnp.bfloat16)
    part_down = norm_factor * jnp.einsum("tr,tk->rk", back_low, acts, preferred_element_type=F32)
    part_up = norm_factor * jnp.einsum("tr,td->rd", low, grads_out, preferred_element_type=F32)
    total = scatter_group(part_down, part_up, y, lax.axis_index("core"))
    total, far, *near = lax.optimization_barrier((total, grads_out, *near))
    blocks = [grads_out, *near, along_y(far, HOPS[3])]
    terms = scatter_rest(total)

    own, near_up, near_down, far = blocks
    from_far, from_up, from_down = product([far, near_up, near_down], w)
    (from_own,) = product([own], w)
    parts = [from_own, along_y(from_up, HOPS[2]), along_y(from_down, HOPS[1]), along_y(from_far, HOPS[3])]
    place = y.astype(jnp.int32)[None]
    grad_down, grad_up = gather_adapter(terms, low.shape[1], hd)
    return finish(place, parts, back_low, down_adapter_matrix), grad_down, grad_up


def solution(mesh):
    fine = Mesh(mesh.devices.reshape(2, 8, 2, 4, 2), ("ylo", "z", "core", "x", "yhi"))
    in_specs = (
        P(TOKENS, None),
        P(TOKENS, None),
        P(("x", "yhi"), ("ylo", "z", "core")),
        P(),
        P(),
    )
    out_specs = (P(TOKENS, None), P(), P())
    return jax.shard_map(local, mesh=fine, in_specs=in_specs, out_specs=out_specs, check_vma=False)
```
